1024 devices in a mesh: dp: 32 (over z_hi, y, core), group: 32 (over x, z_lo).
Axes of the slice: x: 4, y: 8, z: 16 (z_hi: 2, z_lo: 8; z = z_hi * 8 + z_lo), core: 2. Of those that a mesh axis runs over, the one named last changes fastest.
Arguments:
- image_embeds: bfloat16 [16384, 1152], P('dp'), may hold values from -0.1796875 to 0.1796875
- text_embeds: bfloat16 [16384, 1152], P(('dp', 'group')), may hold values from -0.1796875 to 0.1796875
- scale_logarithm: float32 [1], replicated, may hold values from 1.6 to 2.6
- logit_bias: float32 [1], replicated, may hold values from -6 to -2
Outputs:
- image_grads: float32 [16384, 1152], P(('dp', 'group'))
- text_grads: float32 [16384, 1152], P(('dp', 'group'))
The draws below stay inside these ranges and needn't reach their ends.
All inputs are finite; a program needn't handle non-finite values.
Results may differ from the reference program's by a relative error of at most 0.004.
Values may be sent and summed in bfloat16 or wider, within the bound.
A program may use at most 32 MiB of HBM per device.

```python
import jax
import jax.numpy as jnp
from jax import lax

D = 1152
BLOCK = 512
BATCH = 16384
N_DP = 32


def level_of(own_key, shape, shards, low, largest):
    level, own = 1.0, jax.random.fold_in(own_key, 6)
    for dim, blocks in shards:
        steps = jnp.exp(jax.random.uniform(jax.random.fold_in(own, dim), (blocks,), jnp.float32, low / len(shards), largest / len(shards)))
        level = level * jnp.repeat(steps, shape[dim] // blocks).reshape([-1 if axis == dim else 1 for axis in range(len(shape))])
    return level


def gaussian(key, shape, scale, most, shards=(), kind=jnp.bfloat16):
    drawn = scale * jax.random.normal(key, shape, jnp.float32)
    if shards:
        drawn = drawn * level_of(key, shape, shards, -0.22, 0.18)
    return jnp.clip(drawn, -most, most).astype(kind)


def setup_inputs(seed: int = 0) -> dict:
    arg_keys = jax.random.split(jax.random.key(seed), 5)
    return {
        "image_embeds": gaussian(arg_keys[0], (BATCH, D), 0.03, 0.1796875, ((0, 32),)),
        "text_embeds": gaussian(arg_keys[1], (BATCH, D), 0.03, 0.1796875, ((0, 1024),)),
        "scale_logarithm": jnp.clip(jax.random.uniform(arg_keys[2], (1,), jnp.float32, 1.6, 2.6), 1.6, 2.6),
        "logit_bias": jnp.clip(jax.random.uniform(arg_keys[3], (1,), jnp.float32, -6.0, -2.0), -6.0, -2.0),
    }


def normalize(embeds):
    values = embeds.astype(jnp.float32)
    inverse_norm = lax.rsqrt(lax.optimization_barrier(jnp.sum(values * values, axis=1, keepdims=True)) + 1e-06)
    return (values * inverse_norm, inverse_norm)

def norm_backward(unit_rows, unit_grad, inverse_norm):
    along = lax.optimization_barrier(jnp.sum(unit_rows * unit_grad, axis=1, keepdims=True))
    return (unit_grad - unit_rows * along) * inverse_norm

def reference(image_embeds, text_embeds, scale_logarithm, logit_bias):
    scale_factor = jnp.exp(scale_logarithm[0])
    shift_amount = logit_bias[0]
    image_unit, image_norm = normalize(image_embeds)
    text_unit, text_norm = normalize(text_embeds)
    image_half = image_unit.astype(jnp.bfloat16)
    text_second_half = text_unit.astype(jnp.bfloat16)
    block_rows = BLOCK
    text_ids = jnp.arange(BATCH, dtype=jnp.int32)

    def one_block(text_acc, block_index):
        image_row_slice = lax.dynamic_slice_in_dim(image_half, block_index * block_rows, block_rows, 0)
        similarity_matrix = lax.dot_general(image_row_slice, text_second_half, (((1,), (1,)), ((), ())), preferred_element_type=jnp.float32)
        pair_logits = scale_factor * similarity_matrix + shift_amount
        image_ids = block_index * block_rows + jnp.arange(block_rows, dtype=jnp.int32)
        label_sign = jnp.where(image_ids[:, None] == text_ids[None, :], jnp.float32(1.0), jnp.float32(-1.0))
        loss_factor = (-label_sign * jax.nn.sigmoid(-label_sign * pair_logits)).astype(jnp.bfloat16)
        image_portion = scale_factor * jnp.dot(loss_factor, text_second_half, preferred_element_type=jnp.float32)
        text_portion = scale_factor * lax.dot_general(loss_factor, image_row_slice, (((0,), (0,)), ((), ())), preferred_element_type=jnp.float32)
        return (text_acc + text_portion, image_portion)
    start_acc = jnp.zeros((BATCH, D), jnp.float32)
    text_unit_grad, image_parts = lax.scan(one_block, start_acc, jnp.arange(N_DP, dtype=jnp.int32))
    image_unit_grad = image_parts.reshape(BATCH, D)
    image_grads = norm_backward(image_unit, image_unit_grad, image_norm)
    text_grads = norm_backward(text_unit, text_unit_grad, text_norm)
    return (image_grads, text_grads)
```

```python
import jax
import jax.numpy as jnp
from jax import lax
from jax.experimental import pallas as pl
from jax.experimental.pallas import tpu as pltpu
from jax.sharding import PartitionSpec as P

NX = 4
NY = 8
NZ = 8
ROWS = 16

def offsets(count):
    found = [0]
    for distance in range(1, count // 2 + 1):
        found += [distance, -distance]
    return found[:count]


def inverse_norms(values):
    return lax.rsqrt(jnp.sum(values * values, axis=1, keepdims=True) + 1e-06)


def norm_backward(unit_rows, unit_grad, inverse_norm):
    along = jnp.sum(unit_rows * unit_grad, axis=1, keepdims=True)
    return (unit_grad - unit_rows * along) * inverse_norm


def kernel(
    image_hbm, text_ref, scale_ref, bias_ref, image_out, text_out,
    image_in, image_half, texts, coef, coef_text,
    pair_send, pair_recv, text_own, y_send, y_recv, hi_send, hi_recv,
    x_own, x_send, x_recv, z_own, z_send, z_recv,
    in_sem, gather_recv, gather_pair_recv, pair_sem, y_sem, hi_sem, x_sem, z_sem, send_sems,
):
    dp = lax.axis_index("dp")
    group = lax.axis_index("group")
    core = lax.rem(dp, 2)
    y = lax.rem(dp // 2, NY)
    z_hi = dp // (2 * NY)
    x = group // NZ
    z_lo = lax.rem(group, NZ)
    moves = offsets(NY)
    pair_rows = 2 * ROWS
    x_rows = NZ * ROWS

    def dp_at(z_hi, y, core):
        return (z_hi * NY + y) * 2 + core

    sibling = (dp_at(z_hi, y, 1 - core), group)
    opposite = (dp_at(1 - z_hi, y, core), group)

    def y_peer(move):
        return (dp_at(z_hi, lax.rem(y + move + NY, NY), core), group)

    def x_peer(k):
        return (dp, lax.rem(x + k, NX) * NZ + z_lo)

    def z_peer(k):
        return (dp, x * NZ + lax.rem(z_lo + k, NZ))

    load = pltpu.make_async_copy(image_hbm, image_in, in_sem)
    load.start()

    peers = [sibling, opposite]
    peers += [y_peer(move) for move in moves[1:]]
    peers += [x_peer(k) for k in range(1, NX)]
    peers += [z_peer(k) for k in range(1, NZ)]
    barrier = pltpu.get_barrier_semaphore()
    for peer in peers:
        pl.semaphore_signal(barrier, inc=1, device_id=peer, device_id_type=pl.DeviceIdType.MESH)

    text_values = text_ref[...].astype(jnp.float32)
    text_norm = inverse_norms(text_values)
    texts[pl.ds(0, ROWS), :] = (text_values * text_norm).astype(jnp.bfloat16)
    pl.semaphore_wait(barrier, len(peers))

    sent = []

    def send(source, target, arrival, device):
        copy = pltpu.make_async_remote_copy(
            src_ref=source, dst_ref=target, send_sem=send_sems.at[len(sent)], recv_sem=arrival,
            device_id=device, device_id_type=pl.DeviceIdType.MESH,
        )
        copy.start()
        sent.append(copy)
        return copy

    def arrived(target, arrival):
        pltpu.make_async_copy(target, target, arrival).wait()

    def place(p, s, r, count=ROWS):
        return texts.at[pl.ds(p * 4 * ROWS + s * pair_rows + r * ROWS, count), :]

    send(place(0, 0, 0), place(0, 0, 1), gather_recv.at[0, 1], opposite)
    for p in range(NY - 1, 0, -1):
        send(place(0, 0, 0), place(p, 0, 0), gather_recv.at[p, 0], y_peer(moves[p]))
    send(place(0, 0, 0), place(0, 1, 0), gather_pair_recv.at[0, 0], sibling)

    load.wait()

    @pl.loop(0, NX)
    def _(i):
        rows = pl.ds(pl.multiple_of(i * x_rows, x_rows), x_rows)
        values = image_in[rows, :].astype(jnp.float32)
        image_half[rows, :] = (values * inverse_norms(values)).astype(jnp.bfloat16)

    scale_row = jnp.exp(jnp.full((1, image_half.shape[0]), scale_ref[0], jnp.float32))
    bias = bias_ref[0]

    def coefficients(chunk, count):
        start = chunk * count
        logits = lax.dot_general(
            texts[pl.ds(start, count), :], image_half[...], (((1,), (1,)), ((), ())),
            preferred_element_type=jnp.float32,
        ) * scale_row + bias
        if chunk == 0:
            text_ids = lax.broadcasted_iota(jnp.int32, logits.shape, 0)
            image_ids = lax.broadcasted_iota(jnp.int32, logits.shape, 1)
            same = jnp.logical_and(text_ids < ROWS, image_ids == text_ids + group * ROWS)
            sign = jnp.where(same, jnp.float32(1.0), jnp.float32(-1.0))
            values = -sign / (1.0 + jnp.exp(sign * logits))
        else:
            values = 1.0 / (1.0 + jnp.exp(-logits))
        coef_text[pl.ds(start, count), :] = values.astype(jnp.bfloat16)
        coef[:, pl.ds(start, count)] = values.T.astype(jnp.bfloat16)

    arrived(place(0, 0, 1), gather_recv.at[0, 1])
    for p in range(NY - 1, 0, -1):
        send(place(0, 0, 1), place(p, 0, 1), gather_recv.at[p, 1], y_peer(moves[p]))
    send(place(0, 0, 1), place(0, 1, 1), gather_pair_recv.at[0, 1], sibling)

    def take(p):
        if p > 0:
            arrived(place(p, 0, 0), gather_recv.at[p, 0])
            arrived(place(p, 0, 1), gather_recv.at[p, 1])
            send(place(p, 0, 0, pair_rows), place(p, 1, 0, pair_rows), gather_pair_recv.at[p, 0], sibling)

    def take_pair(p):
        if p > 0:
            arrived(place(p, 1, 0, pair_rows), gather_pair_recv.at[p, 0])
        else:
            arrived(place(0, 1, 0), gather_pair_recv.at[0, 0])
            arrived(place(0, 1, 1), gather_pair_recv.at[0, 1])

    chunks = NY // 2
    chunk_rows = 2 * 4 * ROWS
    for chunk in range(chunks + 1):
        if chunk < chunks:
            take(2 * chunk)
            take(2 * chunk + 1)
        if chunk > 0:
            take_pair(2 * chunk - 2)
            take_pair(2 * chunk - 1)
            coefficients(chunk - 1, chunk_rows)

    for k in [2, 1, 3, 0] if NX == 4 else [1, 0]:
        rows = pl.ds(pl.multiple_of(lax.rem(x + k, NX) * x_rows, x_rows), x_rows)
        share = jnp.dot(coef[rows, :], texts[...], preferred_element_type=jnp.float32)
        if k == 0:
            x_own[...] = share
        else:
            x_send[k] = share.astype(jnp.bfloat16)
            send(x_send.at[k], x_recv.at[k], x_sem.at[k], x_peer(k))

    for chunk in range(chunks - 1, -1, -1):
        share = jnp.dot(
            coef_text[pl.ds(chunk * chunk_rows, chunk_rows), :], image_half[...],
            preferred_element_type=jnp.float32,
        )
        for half in range(2):
            p = 2 * chunk + half
            base = half * 4 * ROWS
            text_own[p] = share[base : base + pair_rows]
            pair_send[p] = share[base + pair_rows : base + 2 * pair_rows].astype(jnp.bfloat16)
            send(pair_send.at[p], pair_recv.at[p], pair_sem.at[p], sibling)
    for p in range(NY - 1, -1, -1):
        arrived(pair_recv.at[p], pair_sem.at[p])
        both = text_own[p] + pair_recv[p].astype(jnp.float32)
        if p == 0:
            text_own[0] = both
        else:
            y_send[p] = both.astype(jnp.bfloat16)
            send(y_send.at[p], y_recv.at[p], y_sem.at[p], y_peer(-moves[p]))

    for k in range(1, NX):
        arrived(x_recv.at[k], x_sem.at[k])
    for k in list(range(1, NZ)) + [0]:
        rows = pl.ds(pl.multiple_of(lax.rem(z_lo + k, NZ) * ROWS, ROWS), ROWS)
        total = x_own[rows, :]
        for i in range(1, NX):
            total += x_recv[i, rows, :].astype(jnp.float32)
        if k == 0:
            z_own[...] = total
        else:
            z_send[k] = total.astype(jnp.bfloat16)
            send(z_send.at[k], z_recv.at[k], z_sem.at[k], z_peer(k))

    total = text_own[0]
    for p in range(1, NY):
        arrived(y_recv.at[p], y_sem.at[p])
        total += y_recv[p].astype(jnp.float32)
    hi_send[...] = total[ROWS:].astype(jnp.bfloat16)
    send(hi_send, hi_recv, hi_sem, opposite)
    text_total = total[:ROWS]

    scale = jnp.exp(jnp.full((1, image_in.shape[1]), scale_ref[0], jnp.float32))
    total = z_own[...]
    for k in range(1, NZ):
        arrived(z_recv.at[k], z_sem.at[k])
        total += z_recv[k].astype(jnp.float32)
    own = image_in[pl.ds(pl.multiple_of(group * ROWS, ROWS), ROWS), :].astype(jnp.float32)
    own_norm = inverse_norms(own)
    image_out[...] = norm_backward(own * own_norm, total * scale, own_norm)

    arrived(hi_recv, hi_sem)
    text_total += hi_recv[...].astype(jnp.float32)
    text_out[...] = norm_backward(text_values * text_norm, text_total * scale, text_norm)

    for copy in sent:
        copy.wait_send()


def body(image_embeds, text_embeds, scale_logarithm, logit_bias):
    images, width = image_embeds.shape
    count = NY * 4 * ROWS
    x_rows = NZ * ROWS
    sends = 2 * NY + 1 + NY - 1 + NX - 1 + 2 * NY - 1 + NZ - 1 + 1 + 2
    half = jnp.bfloat16
    dma = pltpu.SemaphoreType.DMA
    return pl.pallas_call(
        kernel,
        out_shape=[jax.ShapeDtypeStruct((ROWS, width), jnp.float32)] * 2,
        in_specs=[
            pl.BlockSpec(memory_space=pl.ANY),
            pl.BlockSpec(memory_space=pltpu.VMEM),
            pl.BlockSpec(memory_space=pltpu.SMEM),
            pl.BlockSpec(memory_space=pltpu.SMEM),
        ],
        out_specs=[pl.BlockSpec(memory_space=pltpu.VMEM)] * 2,
        scratch_shapes=[
            pltpu.VMEM((images, width), half),
            pltpu.VMEM((images, width), half),
            pltpu.VMEM((count, width), half),
            pltpu.VMEM((images, count), half),
            pltpu.VMEM((count, images), half),
            pltpu.VMEM((NY, 2 * ROWS, width), half),
            pltpu.VMEM((NY, 2 * ROWS, width), half),
            pltpu.VMEM((NY, 2 * ROWS, width), jnp.float32),
            pltpu.VMEM((NY, 2 * ROWS, width), half),
            pltpu.VMEM((NY, 2 * ROWS, width), half),
            pltpu.VMEM((ROWS, width), half),
            pltpu.VMEM((ROWS, width), half),
            pltpu.VMEM((x_rows, width), jnp.float32),
            pltpu.VMEM((NX, x_rows, width), half),
            pltpu.VMEM((NX, x_rows, width), half),
            pltpu.VMEM((ROWS, width), jnp.float32),
            pltpu.VMEM((NZ, ROWS, width), half),
            pltpu.VMEM((NZ, ROWS, width), half),
            dma,
            dma((NY, 2)),
            dma((NY, 2)),
            dma((NY,)),
            dma((NY,)),
            dma,
            dma((NX,)),
            dma((NZ,)),
            dma((sends,)),
        ],
        compiler_params=pltpu.CompilerParams(
            collective_id=0, has_side_effects=True, vmem_limit_bytes=48 * 1024 * 1024
        ),
        cost_estimate=pl.CostEstimate(
            flops=6 * images * count * width, bytes_accessed=4 * images * width,
            transcendentals=images * count,
        ),
    )(image_embeds, text_embeds, scale_logarithm, logit_bias)


def solution(mesh):
    return jax.shard_map(
        body,
        mesh=mesh,
        in_specs=(P("dp", None), P(("dp", "group"), None), P(), P()),
        out_specs=(P(("dp", "group"), None), P(("dp", "group"), None)),
        check_vma=False,
    )
```

```python
import jax
import jax.numpy as jnp
from jax import lax
from jax.experimental import pallas as pl
from jax.experimental.pallas import tpu as pltpu
from jax.sharding import PartitionSpec as P

NX = 4
NY = 8
NZ = 8
ROWS = 16
VMEM_BYTES = 56 * 1024 * 1024

def offsets(count):
    found = [0]
    for distance in range(1, count // 2 + 1):
        found += [distance, -distance]
    return found[:count]


def inverse_norms(values):
    return lax.rsqrt(jnp.sum(values * values, axis=1, keepdims=True) + 1e-06)


def norm_backward(unit_rows, unit_grad, inverse_norm):
    along = jnp.sum(unit_rows * unit_grad, axis=1, keepdims=True)
    return (unit_grad - unit_rows * along) * inverse_norm


def kernel(
    image_hbm, text_hbm, scale_hbm, bias_hbm, image_out, text_out,
    image_in, text_in, scale_in, bias_in, image_half, texts, coef, coef_text,
    pair_send, pair_recv, text_own, y_send, y_recv, hi_send, hi_recv,
    x_own, x_send, x_recv, z_own, near_send, near_recv, far_send, far_recv,
    in_sems, gather_recv, gather_pair_recv, pair_sem, y_sem, hi_sem, x_sem, near_sem, far_sem,
    send_sems,
):
    dp = lax.axis_index("dp")
    group = lax.axis_index("group")
    core = lax.rem(dp, 2)
    y = lax.rem(dp // 2, NY)
    z_hi = dp // (2 * NY)
    x = group // NZ
    z_lo = lax.rem(group, NZ)
    z_pair = z_lo // 2
    z_side = lax.rem(z_lo, 2)
    moves = offsets(NY)
    pairs = NZ // 2
    x_rows = NZ * ROWS
    pair_rows = 2 * ROWS

    def dp_at(z_hi, y, core):
        return (z_hi * NY + y) * 2 + core

    sibling = (dp_at(z_hi, y, 1 - core), group)
    opposite = (dp_at(1 - z_hi, y, core), group)
    near = (dp, x * NZ + z_pair * 2 + 1 - z_side)

    def y_peer(move):
        return (dp_at(z_hi, lax.rem(y + move + NY, NY), core), group)

    def x_peer(k):
        return (dp, lax.rem(x + k, NX) * NZ + z_lo)

    def far_peer(j):
        return (dp, x * NZ + lax.rem(z_pair + j, pairs) * 2 + z_side)

    loads = [
        pltpu.make_async_copy(source, target, in_sems.at[i])
        for i, (source, target) in enumerate(
            [(text_hbm, text_in), (image_hbm, image_in), (scale_hbm, scale_in), (bias_hbm, bias_in)]
        )
    ]
    for load in loads:
        load.start()

    peers = [opposite, sibling, near]
    peers += [y_peer(move) for move in moves[1:]]
    peers += [x_peer(k) for k in range(1, NX)]
    peers += [far_peer(j) for j in range(1, pairs)]
    barrier = pltpu.get_barrier_semaphore()
    for peer in peers:
        pl.semaphore_signal(barrier, inc=1, device_id=peer, device_id_type=pl.DeviceIdType.MESH)

    loads[0].wait()
    text_values = text_in[...].astype(jnp.float32)
    text_norm = inverse_norms(text_values)
    texts[pl.ds(0, ROWS), :] = (text_values * text_norm).astype(jnp.bfloat16)
    pl.semaphore_wait(barrier, len(peers))

    sent = []

    def send(source, target, arrival, device):
        copy = pltpu.make_async_remote_copy(
            src_ref=source, dst_ref=target, send_sem=send_sems.at[len(sent)], recv_sem=arrival,
            device_id=device, device_id_type=pl.DeviceIdType.MESH,
        )
        copy.start()
        sent.append(copy)

    def arrived(target, arrival):
        pltpu.make_async_copy(target, target, arrival).wait()

    def place(r, p, s):
        return texts.at[pl.ds((r * NY + p) * pair_rows + s * ROWS, ROWS), :]

    def forward(r):
        for p in range(NY - 1, 0, -1):
            send(place(r, 0, 0), place(r, p, 0), gather_recv.at[r, p], y_peer(moves[p]))
        send(place(r, 0, 0), place(r, 0, 1), gather_pair_recv.at[r, 0], sibling)

    def take(r, places):
        for p in places:
            if p > 0:
                arrived(place(r, p, 0), gather_recv.at[r, p])
                send(place(r, p, 0), place(r, p, 1), gather_pair_recv.at[r, p], sibling)

    def take_pair(r, places):
        for p in places:
            arrived(place(r, p, 1), gather_pair_recv.at[r, p])

    send(place(0, 0, 0), place(1, 0, 0), gather_recv.at[1, 0], opposite)
    forward(0)

    for load in loads[1:]:
        load.wait()

    @pl.loop(0, NX)
    def _(i):
        rows = pl.ds(pl.multiple_of(i * x_rows, x_rows), x_rows)
        values = image_in[rows, :].astype(jnp.float32)
        image_half[rows, :] = (values * inverse_norms(values)).astype(jnp.bfloat16)

    scale_row = jnp.exp(jnp.full((1, image_half.shape[0]), scale_in[0], jnp.float32))
    bias = bias_in[0]
    some = NY // 2
    some_rows = some * pair_rows

    def coefficients(r, half):
        start = (2 * r + half) * some_rows
        logits = lax.dot_general(
            texts[pl.ds(start, some_rows), :], image_half[...], (((1,), (1,)), ((), ())),
            preferred_element_type=jnp.float32,
        ) * scale_row + bias
        if start == 0:
            text_ids = lax.broadcasted_iota(jnp.int32, logits.shape, 0)
            image_ids = lax.broadcasted_iota(jnp.int32, logits.shape, 1)
            same = jnp.logical_and(text_ids < ROWS, image_ids == text_ids + group * ROWS)
            sign = jnp.where(same, jnp.float32(1.0), jnp.float32(-1.0))
            values = -sign / (1.0 + jnp.exp(sign * logits))
        else:
            values = 1.0 / (1.0 + jnp.exp(-logits))
        coef_text[pl.ds(start, some_rows), :] = values.astype(jnp.bfloat16)
        coef[:, pl.ds(start, some_rows)] = values.T.astype(jnp.bfloat16)

    def text_share(r, half):
        share = jnp.dot(
            coef_text[pl.ds((2 * r + half) * some_rows, some_rows), :], image_half[...],
            preferred_element_type=jnp.float32,
        )
        for i in range(some):
            base = i * pair_rows
            text_own[r, half * some + i] = share[base : base + ROWS]
            pair_send[r, half, i] = share[base + ROWS : base + pair_rows].astype(jnp.bfloat16)
        send(pair_send.at[r, half], pair_recv.at[r, half], pair_sem.at[r, half], sibling)

    def pair_sum(r):
        for half in range(1, -1, -1):
            arrived(pair_recv.at[r, half], pair_sem.at[r, half])
            for i in range(some - 1, -1, -1):
                p = half * some + i
                both = text_own[r, p] + pair_recv[r, half, i].astype(jnp.float32)
                if p == 0:
                    text_own[r, 0] = both
                else:
                    y_send[r, p] = both.astype(jnp.bfloat16)

    def y_sends(r):
        for p in range(NY - 1, 0, -1):
            send(y_send.at[r, p], y_recv.at[r, p], y_sem.at[r, p], y_peer(-moves[p]))

    def y_sum(r):
        total = text_own[r, 0]
        for p in range(1, NY):
            arrived(y_recv.at[r, p], y_sem.at[r, p])
            total += y_recv[r, p].astype(jnp.float32)
        return total

    def image_share(k):
        rows = pl.ds(pl.multiple_of(lax.rem(x + k, NX) * x_rows, x_rows), x_rows)
        share = jnp.dot(coef[rows, :], texts[...], preferred_element_type=jnp.float32)
        if k == 0:
            x_own[...] = share
        else:
            x_send[k] = share.astype(jnp.bfloat16)

    def piece_rows(j):
        return pl.ds(pl.multiple_of(lax.rem(z_pair + j, pairs) * pair_rows, pair_rows), pair_rows)

    def x_sends(j, k):
        send(x_send.at[k, piece_rows(j), :], x_recv.at[j, k], x_sem.at[j, k], x_peer(k))

    def x_sum(j):
        total = x_own[piece_rows(j), :]
        for k in range(1, NX):
            arrived(x_recv.at[j, k], x_sem.at[j, k])
            total += x_recv[j, k].astype(jnp.float32)
        z_own[j] = total
        theirs = pl.ds(pl.multiple_of((1 - z_side) * ROWS, ROWS), ROWS)
        near_send[j] = z_own[j, theirs, :].astype(jnp.bfloat16)
        send(near_send.at[j], near_recv.at[j], near_sem.at[j], near)

    def near_sum(j):
        arrived(near_recv.at[j], near_sem.at[j])
        ours = pl.ds(pl.multiple_of(z_side * ROWS, ROWS), ROWS)
        return z_own[j, ours, :] + near_recv[j].astype(jnp.float32)

    def far_sends(j):
        far_send[j] = near_sum(j).astype(jnp.bfloat16)
        send(far_send.at[j], far_recv.at[j], far_sem.at[j], far_peer(j))

    first, second = range(some), range(some, NY)
    take(0, range(NY))
    arrived(place(1, 0, 0), gather_recv.at[1, 0])
    forward(1)
    for half, places in enumerate((first, second)):
        take_pair(0, places)
        coefficients(0, half)
    text_share(0, 0)
    text_share(0, 1)
    take(1, first)
    take(1, second[: some // 2])
    take_pair(1, first)
    coefficients(1, 0)
    text_share(1, 0)
    pair_sum(0)
    take(1, second[some // 2 :])
    take_pair(1, second)
    coefficients(1, 1)
    text_share(1, 1)

    x_order = [2, 1, 3] if NX == 4 else list(range(1, NX))
    j_order = [2, 1, 3, 0] if pairs == 4 else list(range(pairs - 1, -1, -1))
    image_share(x_order[0])
    x_sends(j_order[0], x_order[0])
    pair_sum(1)
    y_sends(1)
    for k in x_order[1:]:
        image_share(k)
        x_sends(j_order[0], k)
    for j in j_order[1:]:
        for k in x_order:
            x_sends(j, k)
    y_sends(0)
    image_share(0)

    x_sum(j_order[0])
    hi_send[...] = y_sum(1).astype(jnp.bfloat16)
    send(hi_send, hi_recv, hi_sem, opposite)
    for before, j in zip(j_order, j_order[1:]):
        x_sum(j)
        far_sends(before)
    text_total = y_sum(0)
    total = near_sum(0)
    for j in j_order[:-1]:
        arrived(far_recv.at[j], far_sem.at[j])
        total += far_recv[j].astype(jnp.float32)
    scale = jnp.exp(jnp.full((1, image_in.shape[1]), scale_in[0], jnp.float32))
    own = image_in[pl.ds(pl.multiple_of(group * ROWS, ROWS), ROWS), :].astype(jnp.float32)
    own_norm = inverse_norms(own)
    image_out[...] = norm_backward(own * own_norm, total * scale, own_norm)

    arrived(hi_recv, hi_sem)
    text_total += hi_recv[...].astype(jnp.float32)
    text_out[...] = norm_backward(text_values * text_norm, text_total * scale, text_norm)

    for copy in sent:
        copy.wait_send()


def body(image_embeds, text_embeds, scale_logarithm, logit_bias):
    images, width = image_embeds.shape
    count = NY * 4 * ROWS
    x_rows = NZ * ROWS
    pairs = NZ // 2
    sends = 1 + 4 * NY - 2 + 4 + 2 * NY - 2 + pairs * (NX - 1) + 2 * pairs - 1 + 1 + 2
    dma = pltpu.SemaphoreType.DMA

    def half(*shape):
        return pltpu.VMEM((*shape, width), jnp.bfloat16)

    def full(*shape):
        return pltpu.VMEM((*shape, width), jnp.float32)

    return pl.pallas_call(
        kernel,
        out_shape=[jax.ShapeDtypeStruct((ROWS, width), jnp.float32)] * 2,
        in_specs=[pl.BlockSpec(memory_space=pl.ANY)] * 4,
        out_specs=[pl.BlockSpec(memory_space=pltpu.VMEM)] * 2,
        scratch_shapes=[
            half(images),
            half(ROWS),
            pltpu.SMEM((1,), jnp.float32),
            pltpu.SMEM((1,), jnp.float32),
            half(images),
            half(count),
            pltpu.VMEM((images, count), jnp.bfloat16),
            pltpu.VMEM((count, images), jnp.bfloat16),
            half(2, 2, NY // 2, ROWS),
            half(2, 2, NY // 2, ROWS),
            full(2, NY, ROWS),
            half(2, NY, ROWS),
            half(2, NY, ROWS),
            half(ROWS),
            half(ROWS),
            full(x_rows),
            half(NX, x_rows),
            half(pairs, NX, 2 * ROWS),
            full(pairs, 2 * ROWS),
            half(pairs, ROWS),
            half(pairs, ROWS),
            half(pairs, ROWS),
            half(pairs, ROWS),
            dma((4,)),
            dma((2, NY)),
            dma((2, NY)),
            dma((2, 2)),
            dma((2, NY)),
            dma,
            dma((pairs, NX)),
            dma((pairs,)),
            dma((pairs,)),
            dma((sends,)),
        ],
        compiler_params=pltpu.CompilerParams(
            collective_id=0, has_side_effects=True, vmem_limit_bytes=VMEM_BYTES
        ),
        cost_estimate=pl.CostEstimate(
            flops=6 * images * count * width, bytes_accessed=4 * images * width,
            transcendentals=images * count,
        ),
    )(image_embeds, text_embeds, scale_logarithm, logit_bias)


def solution(mesh):
    return jax.shard_map(
        body,
        mesh=mesh,
        in_specs=(P("dp", None), P(("dp", "group"), None), P(), P()),
        out_specs=(P(("dp", "group"), None), P(("dp", "group"), None)),
        check_vma=False,
    )
```

```python
import jax
import jax.numpy as jnp
from jax import lax
from jax.experimental import pallas as pl
from jax.experimental.pallas import tpu as pltpu
from jax.sharding import PartitionSpec as P

NX = 4
NY = 8
NZ = 8
ROWS = 16
VMEM_BYTES = 53 * 1024 * 1024 + 512 * 1024

def offsets(count):
    found = [0]
    for distance in range(1, count // 2 + 1):
        found += [distance, -distance]
    return found[:count]


def inverse_norms(values):
    return lax.rsqrt(jnp.sum(values * values, axis=1, keepdims=True) + 1e-06)


def norm_backward(unit_rows, unit_grad, inverse_norm):
    along = jnp.sum(unit_rows * unit_grad, axis=1, keepdims=True)
    return (unit_grad - unit_rows * along) * inverse_norm


def kernel(
    image_hbm, text_hbm, scale_hbm, bias_hbm, image_out, text_out,
    image_in, text_in, scale_in, bias_in, image_half, texts, coef, coef_text,
    pair_send, pair_recv, text_own, y_send, y_recv, hi_send, hi_recv,
    x_full, x_half, pass_send, pass_recv, x_recv, z_own, near_send, near_recv, far_send, far_recv,
    in_sems, gather_recv, gather_pair_recv, pair_sem, y_sem, hi_sem, pass_sem, x_sem, near_sem, far_sem,
    send_sems,
):
    dp = lax.axis_index("dp")
    group = lax.axis_index("group")
    core = lax.rem(dp, 2)
    y = lax.rem(dp // 2, NY)
    z_hi = dp // (2 * NY)
    x = group // NZ
    z_lo = lax.rem(group, NZ)
    z_pair = z_lo // 2
    z_side = lax.rem(z_lo, 2)
    moves = offsets(NY)
    pairs = NZ // 2
    x_rows = NZ * ROWS
    pair_rows = 2 * ROWS

    def dp_at(z_hi, y, core):
        return (z_hi * NY + y) * 2 + core

    sibling = (dp_at(z_hi, y, 1 - core), group)
    opposite = (dp_at(1 - z_hi, y, core), group)
    near = (dp, x * NZ + z_pair * 2 + 1 - z_side)

    def y_peer(move):
        return (dp_at(z_hi, lax.rem(y + move + NY, NY), core), group)

    def x_peer(k):
        return (dp, lax.rem(x + k, NX) * NZ + z_lo)

    def pair_at(j):
        low, high = lax.rem(z_pair, 2), z_pair // 2
        low = low if j % 2 == 0 else 1 - low
        high = high if j < 2 else 1 - high
        return high * 2 + low

    def far_peer(j):
        return (dp, x * NZ + pair_at(j) * 2 + z_side)

    loads = [
        pltpu.make_async_copy(source, target, in_sems.at[i])
        for i, (source, target) in enumerate(
            [(text_hbm, text_in), (image_hbm, image_in), (scale_hbm, scale_in), (bias_hbm, bias_in)]
        )
    ]
    for load in loads:
        load.start()

    peers = [opposite, sibling, near]
    peers += [y_peer(move) for move in moves[1:5]]
    peers += [x_peer(1), x_peer(3)]
    peers += [far_peer(1), far_peer(2)]
    barrier = pltpu.get_barrier_semaphore()
    for peer in peers:
        pl.semaphore_signal(barrier, inc=1, device_id=peer, device_id_type=pl.DeviceIdType.MESH)

    loads[0].wait()
    text_values = text_in[...].astype(jnp.float32)
    text_norm = inverse_norms(text_values)
    texts[pl.ds(0, ROWS), :] = (text_values * text_norm).astype(jnp.bfloat16)

    for load in loads[1:]:
        load.wait()

    @pl.loop(0, NX)
    def _(i):
        rows = pl.ds(pl.multiple_of(i * x_rows, x_rows), x_rows)
        values = image_in[rows, :].astype(jnp.float32)
        image_half[rows, :] = (values * inverse_norms(values)).astype(jnp.bfloat16)

    pl.semaphore_wait(barrier, len(peers))

    started, pending = [], {}

    def send(source, target, arrival, device):
        copy = pltpu.make_async_remote_copy(
            src_ref=source, dst_ref=target, send_sem=send_sems.at[len(started)], recv_sem=arrival,
            device_id=device, device_id_type=pl.DeviceIdType.MESH,
        )
        copy.start()
        pending[len(started)] = copy
        started.append(copy)
        return len(started) - 1

    def arrived(target, arrival):
        pltpu.make_async_copy(target, target, arrival).wait()

    def place(r, p, s):
        start = (r * NY + p) * pair_rows + s * ROWS
        return texts.at[pl.ds(start if isinstance(start, int) else pl.multiple_of(start, ROWS), ROWS), :]

    def gather_send(r, source, target, move):
        send(place(r, source, 0), place(r, target, 0), gather_recv.at[r, target], y_peer(move))

    def forward(r):
        for p in (3, 4, 1, 2):
            gather_send(r, 0, p, moves[p])
        send(place(r, 0, 0), place(r, 0, 1), gather_pair_recv.at[r, 0], sibling)

    def take(r, places):
        for p in places:
            arrived(place(r, p, 0), gather_recv.at[r, p])
            if p == 3:
                gather_send(r, 3, 5, 1)
            elif p == 4:
                gather_send(r, 4, 6, -1)
                gather_send(r, 3 + core, 7, 2 - 4 * core)
            send(place(r, p, 0), place(r, p, 1), gather_pair_recv.at[r, p], sibling)

    def take_pair(r, places):
        for p in places:
            arrived(place(r, p, 1), gather_pair_recv.at[r, p])

    send(place(0, 0, 0), place(1, 0, 0), gather_recv.at[1, 0], opposite)
    forward(0)

    scale_row = jnp.exp(jnp.full((1, image_half.shape[0]), scale_in[0], jnp.float32))
    bias = bias_in[0]
    some = NY // 2
    some_rows = some * pair_rows

    def coefficients(r, half):
        start = (2 * r + half) * some_rows
        logits = lax.dot_general(
            texts[pl.ds(start, some_rows), :], image_half[...], (((1,), (1,)), ((), ())),
            preferred_element_type=jnp.float32,
        ) * scale_row + bias
        if start == 0:
            text_ids = lax.broadcasted_iota(jnp.int32, logits.shape, 0)
            image_ids = lax.broadcasted_iota(jnp.int32, logits.shape, 1)
            same = jnp.logical_and(text_ids < ROWS, image_ids == text_ids + group * ROWS)
            sign = jnp.where(same, jnp.float32(1.0), jnp.float32(-1.0))
            values = -sign / (1.0 + jnp.exp(sign * logits))
        else:
            values = 1.0 / (1.0 + jnp.exp(-logits))
        coef_text[pl.ds(start, some_rows), :] = values.astype(jnp.bfloat16)
        coef[:, pl.ds(start, some_rows)] = values.T.astype(jnp.bfloat16)

    def text_share(r, half):
        share = jnp.dot(
            coef_text[pl.ds((2 * r + half) * some_rows, some_rows), :], image_half[...],
            preferred_element_type=jnp.float32,
        )
        for i in range(some):
            base = i * pair_rows
            text_own[r, half * some + i] = share[base : base + ROWS]
            pair_send[r, half, i] = share[base + ROWS : base + pair_rows].astype(jnp.bfloat16)
        send(pair_send.at[r, half], pair_recv.at[r, half], pair_sem.at[r, half], sibling)

    def pair_sum(r):
        for half in range(1, -1, -1):
            arrived(pair_recv.at[r, half], pair_sem.at[r, half])
            for i in range(some - 1, -1, -1):
                p = half * some + i
                both = text_own[r, p] + pair_recv[r, half, i].astype(jnp.float32)
                if p in (0, 3, 4):
                    text_own[r, p] = both
                else:
                    y_send[r, p] = both.astype(jnp.bfloat16)

    def y_send_to(r, p, move):
        send(y_send.at[r, p], y_recv.at[r, p], y_sem.at[r, p], y_peer(move))

    def y_first(r):
        y_send_to(r, 7, 2 - 4 * core)
        y_send_to(r, 6, 1)
        y_send_to(r, 5, -1)
        y_send_to(r, 2, 1)
        y_send_to(r, 1, -1)

    def y_pass(r):
        for p in (5, 6, 7):
            arrived(y_recv.at[r, p], y_sem.at[r, p])
        last = y_recv[r, 7].astype(jnp.float32)
        for p in (3, 4):
            both = text_own[r, p] + y_recv[r, p + 2].astype(jnp.float32)
            both += jnp.where(core == 4 - p, last, jnp.zeros_like(last))
            y_send[r, p] = both.astype(jnp.bfloat16)
            y_send_to(r, p, -moves[p])

    def y_sum(r):
        total = text_own[r, 0]
        for p in range(1, 5):
            arrived(y_recv.at[r, p], y_sem.at[r, p])
            total += y_recv[r, p].astype(jnp.float32)
        return total

    def image_share(k):
        rows = pl.ds(pl.multiple_of(lax.rem(x + k, NX) * x_rows, x_rows), x_rows)
        share = jnp.dot(coef[rows, :], texts[...], preferred_element_type=jnp.float32)
        if k != 2:
            x_full[k] = share
        if k != 0:
            x_half[k] = share.astype(jnp.bfloat16)

    def side_rows(j, side):
        start = (pair_at(j) * 2 + side) * ROWS
        return pl.ds(pl.multiple_of(start, ROWS), ROWS)

    def pass_sends(j):
        for way in range(2):
            send(
                x_half.at[2, side_rows(j, way), :], pass_recv.at[j, way], pass_sem.at[j, way],
                x_peer(1 + 2 * way),
            )

    going = [[] for _ in range(pairs)]

    def x_sends(j):
        for way in range(2):
            going[j].append(send(
                x_half.at[1 + 2 * way, side_rows(j, 1 - way), :], x_recv.at[j, way, 1 - way],
                x_sem.at[j, way, 1 - way], x_peer(1 + 2 * way),
            ))
        for way in range(2):
            arrived(pass_recv.at[j, way], pass_sem.at[j, way])
            both = x_full[1 + 2 * way, side_rows(j, way), :] + pass_recv[j, way].astype(jnp.float32)
            pass_send[j, way] = both.astype(jnp.bfloat16)
            going[j].append(send(
                pass_send.at[j, way], x_recv.at[j, way, way], x_sem.at[j, way, way],
                x_peer(1 + 2 * way),
            ))

    def settle(j):
        for index in going[j]:
            pending.pop(index).wait_send()

    def x_sum(j):
        for side in range(2):
            total = x_full[0, side_rows(j, side), :]
            for way in range(2):
                arrived(x_recv.at[j, way, side], x_sem.at[j, way, side])
                total += x_recv[j, way, side].astype(jnp.float32)
            z_own[j, side] = total
        near_send[j] = z_own[j, 1 - z_side].astype(jnp.bfloat16)
        send(near_send.at[j], near_recv.at[j], near_sem.at[j], near)

    def near_sum(j):
        arrived(near_recv.at[j], near_sem.at[j])
        return z_own[j, z_side] + near_recv[j].astype(jnp.float32)

    def middle_sends(j):
        far_send[j] = near_sum(j).astype(jnp.bfloat16)
        send(far_send.at[j], far_recv.at[j], far_sem.at[j], far_peer(1))

    def far_sends():
        total = near_sum(2)
        arrived(far_recv.at[3], far_sem.at[3])
        far_send[2] = (total + far_recv[3].astype(jnp.float32)).astype(jnp.bfloat16)
        send(far_send.at[2], far_recv.at[2], far_sem.at[2], far_peer(2))

    first, second = range(some), range(some, NY)
    order = (3, 4, 1, 2)
    rest = (5, 6, 7)
    take(0, order)
    arrived(place(1, 0, 0), gather_recv.at[1, 0])
    forward(1)
    take(0, rest)
    take(1, order)
    for half, places in enumerate((first, second)):
        take_pair(0, places)
        coefficients(0, half)
        text_share(0, half)
    take(1, rest)
    take_pair(1, first)
    coefficients(1, 0)
    text_share(1, 0)
    take_pair(1, second)
    coefficients(1, 1)
    text_share(1, 1)

    image_share(2)
    pass_sends(3)
    pass_sends(2)
    pair_sum(1)
    y_first(1)
    image_share(1)
    image_share(3)
    x_sends(3)
    pass_sends(1)
    pair_sum(0)
    image_share(0)
    y_pass(1)
    x_sends(2)
    settle(3)
    pass_sends(0)
    x_sends(1)
    y_first(0)
    x_sum(3)
    settle(2)
    x_sends(0)
    hi_send[...] = y_sum(1).astype(jnp.bfloat16)
    send(hi_send, hi_recv, hi_sem, opposite)
    x_sum(2)
    middle_sends(3)
    y_pass(0)
    x_sum(1)
    far_sends()
    middle_sends(1)
    x_sum(0)
    text_total = y_sum(0)
    total = near_sum(0)
    for j in (1, 2):
        arrived(far_recv.at[j], far_sem.at[j])
        total += far_recv[j].astype(jnp.float32)
    scale = jnp.exp(jnp.full((1, image_in.shape[1]), scale_in[0], jnp.float32))
    own = image_in[pl.ds(pl.multiple_of(group * ROWS, ROWS), ROWS), :].astype(jnp.float32)
    own_norm = inverse_norms(own)
    image_out[...] = norm_backward(own * own_norm, total * scale, own_norm)

    arrived(hi_recv, hi_sem)
    text_total += hi_recv[...].astype(jnp.float32)
    text_out[...] = norm_backward(text_values * text_norm, text_total * scale, text_norm)

    for copy in pending.values():
        copy.wait_send()


def body(image_embeds, text_embeds, scale_logarithm, logit_bias):
    images, width = image_embeds.shape
    count = NY * 4 * ROWS
    x_rows = NZ * ROWS
    pairs = NZ // 2
    sends = 1 + 4 * NY - 2 + 4 + 2 * NY - 2 + 6 * pairs + 2 * pairs - 1 + 1
    dma = pltpu.SemaphoreType.DMA

    def half(*shape):
        return pltpu.VMEM((*shape, width), jnp.bfloat16)

    def full(*shape):
        return pltpu.VMEM((*shape, width), jnp.float32)

    return pl.pallas_call(
        kernel,
        out_shape=[jax.ShapeDtypeStruct((ROWS, width), jnp.float32)] * 2,
        in_specs=[pl.BlockSpec(memory_space=pl.ANY)] * 4,
        out_specs=[pl.BlockSpec(memory_space=pltpu.VMEM)] * 2,
        scratch_shapes=[
            half(images),
            half(ROWS),
            pltpu.SMEM((1,), jnp.float32),
            pltpu.SMEM((1,), jnp.float32),
            half(images),
            half(count),
            pltpu.VMEM((images, count), jnp.bfloat16),
            pltpu.VMEM((count, images), jnp.bfloat16),
            half(2, 2, NY // 2, ROWS),
            half(2, 2, NY // 2, ROWS),
            full(2, NY, ROWS),
            half(2, NY, ROWS),
            half(2, NY, ROWS),
            half(ROWS),
            half(ROWS),
            full(NX, x_rows),
            half(NX, x_rows),
            half(pairs, 2, ROWS),
            half(pairs, 2, ROWS),
            half(pairs, 2, 2, ROWS),
            full(pairs, 2, ROWS),
            half(pairs, ROWS),
            half(pairs, ROWS),
            half(pairs, ROWS),
            half(pairs, ROWS),
            dma((4,)),
            dma((2, NY)),
            dma((2, NY)),
            dma((2, 2)),
            dma((2, NY)),
            dma,
            dma((pairs, 2)),
            dma((pairs, 2, 2)),
            dma((pairs,)),
            dma((pairs,)),
            dma((sends,)),
        ],
        compiler_params=pltpu.CompilerParams(
            collective_id=0, has_side_effects=True, vmem_limit_bytes=VMEM_BYTES
        ),
        cost_estimate=pl.CostEstimate(
            flops=6 * images * count * width, bytes_accessed=4 * images * width,
            transcendentals=images * count,
        ),
    )(image_embeds, text_embeds, scale_logarithm, logit_bias)


def solution(mesh):
    return jax.shard_map(
        body,
        mesh=mesh,
        in_specs=(P("dp", None), P(("dp", "group"), None), P(), P()),
        out_specs=(P(("dp", "group"), None), P(("dp", "group"), None)),
        check_vma=False,
    )
```

```python
import jax
import jax.numpy as jnp
from jax import lax
from jax.experimental import pallas as pl
from jax.experimental.pallas import tpu as pltpu
from jax.sharding import PartitionSpec as P

NX = 4
NY = 8
NZ = 8
ROWS = 16
VMEM_BYTES = 53 * 1024 * 1024 + 512 * 1024

def offsets(count):
    found = [0]
    for distance in range(1, count // 2 + 1):
        found += [distance, -distance]
    return found[:count]


def inverse_norms(values):
    return lax.rsqrt(jnp.sum(values * values, axis=1, keepdims=True) + 1e-06)


def norm_backward(unit_rows, unit_grad, inverse_norm):
    along = jnp.sum(unit_rows * unit_grad, axis=1, keepdims=True)
    return (unit_grad - unit_rows * along) * inverse_norm


def kernel(
    image_hbm, text_hbm, scale_hbm, bias_hbm, image_out, text_out,
    image_in, text_in, scale_in, bias_in, image_half, texts, coef, coef_text,
    pair_send, pair_recv, text_own, y_send, y_recv, hi_send, hi_recv,
    x_full, x_half, pass_send, pass_recv, x_recv, z_own, near_send, near_recv, far_send, far_recv,
    in_sems, gather_recv, gather_pair_recv, pair_sem, y_sem, hi_sem, pass_sem, x_sem, near_sem, far_sem,
    send_sems,
):
    dp = lax.axis_index("dp")
    group = lax.axis_index("group")
    core = lax.rem(dp, 2)
    y = lax.rem(dp // 2, NY)
    z_hi = dp // (2 * NY)
    x = group // NZ
    z_lo = lax.rem(group, NZ)
    z_pair = z_lo // 2
    z_side = lax.rem(z_lo, 2)
    moves = offsets(NY)
    pairs = NZ // 2
    x_rows = NZ * ROWS
    pair_rows = 2 * ROWS

    def dp_at(z_hi, y, core):
        return (z_hi * NY + y) * 2 + core

    sibling = (dp_at(z_hi, y, 1 - core), group)
    opposite = (dp_at(1 - z_hi, y, core), group)
    near = (dp, x * NZ + z_pair * 2 + 1 - z_side)

    def y_peer(move):
        return (dp_at(z_hi, lax.rem(y + move + NY, NY), core), group)

    def x_peer(k):
        return (dp, lax.rem(x + k, NX) * NZ + z_lo)

    def pair_at(j):
        low, high = lax.rem(z_pair, 2), z_pair // 2
        low = low if j % 2 == 0 else 1 - low
        high = high if j < 2 else 1 - high
        return high * 2 + low

    def far_peer(j):
        return (dp, x * NZ + pair_at(j) * 2 + z_side)

    peers = [opposite, sibling, near]
    peers += [y_peer(move) for move in moves[1:5]]
    peers += [x_peer(1), x_peer(3)]
    peers += [far_peer(1), far_peer(2)]
    barrier = pltpu.get_barrier_semaphore()
    for peer in peers:
        pl.semaphore_signal(barrier, inc=1, device_id=peer, device_id_type=pl.DeviceIdType.MESH)

    loads = [
        pltpu.make_async_copy(source, target, in_sems.at[i])
        for i, (source, target) in enumerate(
            [(text_hbm, text_in), (image_hbm, image_in), (scale_hbm, scale_in), (bias_hbm, bias_in)]
        )
    ]
    for load in loads:
        load.start()

    loads[0].wait()
    text_values = text_in[...].astype(jnp.float32)
    text_norm = inverse_norms(text_values)
    texts[pl.ds(0, ROWS), :] = (text_values * text_norm).astype(jnp.bfloat16)

    for load in loads[1:]:
        load.wait()

    @pl.loop(0, NX)
    def _(i):
        rows = pl.ds(pl.multiple_of(i * x_rows, x_rows), x_rows)
        values = image_in[rows, :].astype(jnp.float32)
        image_half[rows, :] = (values * inverse_norms(values)).astype(jnp.bfloat16)

    pl.semaphore_wait(barrier, len(peers))

    sent = []

    def send(source, target, arrival, device):
        copy = pltpu.make_async_remote_copy(
            src_ref=source, dst_ref=target, send_sem=send_sems.at[len(sent)], recv_sem=arrival,
            device_id=device, device_id_type=pl.DeviceIdType.MESH,
        )
        copy.start()
        sent.append(copy)

    def arrived(target, arrival):
        pltpu.make_async_copy(target, target, arrival).wait()

    def place(r, p, s):
        start = (r * NY + p) * pair_rows + s * ROWS
        return texts.at[pl.ds(start if isinstance(start, int) else pl.multiple_of(start, ROWS), ROWS), :]

    def gather_send(r, source, target, move):
        send(place(r, source, 0), place(r, target, 0), gather_recv.at[r, target], y_peer(move))

    def forward(r):
        for p in (3, 4, 1, 2):
            gather_send(r, 0, p, moves[p])
        send(place(r, 0, 0), place(r, 0, 1), gather_pair_recv.at[r, 0], sibling)

    def take(r, places):
        for p in places:
            arrived(place(r, p, 0), gather_recv.at[r, p])
            if p == 3:
                gather_send(r, 3, 5, 1)
            elif p == 4:
                gather_send(r, 4, 6, -1)
                gather_send(r, 3 + core, 7, 2 - 4 * core)
            send(place(r, p, 0), place(r, p, 1), gather_pair_recv.at[r, p], sibling)

    def take_pair(r, places):
        for p in places:
            arrived(place(r, p, 1), gather_pair_recv.at[r, p])

    send(place(0, 0, 0), place(1, 0, 0), gather_recv.at[1, 0], opposite)
    forward(0)

    scale_row = jnp.exp(jnp.full((1, image_half.shape[0]), scale_in[0], jnp.float32))
    bias = bias_in[0]
    some = NY // 2
    some_rows = some * pair_rows

    def coefficients(r, half):
        start = (2 * r + half) * some_rows
        logits = lax.dot_general(
            texts[pl.ds(start, some_rows), :], image_half[...], (((1,), (1,)), ((), ())),
            preferred_element_type=jnp.float32,
        ) * scale_row + bias
        if start == 0:
            text_ids = lax.broadcasted_iota(jnp.int32, logits.shape, 0)
            image_ids = lax.broadcasted_iota(jnp.int32, logits.shape, 1)
            same = jnp.logical_and(text_ids < ROWS, image_ids == text_ids + group * ROWS)
            sign = jnp.where(same, jnp.float32(1.0), jnp.float32(-1.0))
            values = -sign / (1.0 + jnp.exp(sign * logits))
        else:
            values = 1.0 / (1.0 + jnp.exp(-logits))
        coef_text[pl.ds(start, some_rows), :] = values.astype(jnp.bfloat16)
        coef[:, pl.ds(start, some_rows)] = values.T.astype(jnp.bfloat16)

    def text_share(r, half):
        share = jnp.dot(
            coef_text[pl.ds((2 * r + half) * some_rows, some_rows), :], image_half[...],
            preferred_element_type=jnp.float32,
        )
        for i in range(some):
            base = i * pair_rows
            text_own[r, half * some + i] = share[base : base + ROWS]
            pair_send[r, half, i] = share[base + ROWS : base + pair_rows].astype(jnp.bfloat16)
        send(pair_send.at[r, half], pair_recv.at[r, half], pair_sem.at[r, half], sibling)

    def pair_sum(r):
        for half in range(1, -1, -1):
            arrived(pair_recv.at[r, half], pair_sem.at[r, half])
            for i in range(some - 1, -1, -1):
                p = half * some + i
                both = text_own[r, p] + pair_recv[r, half, i].astype(jnp.float32)
                if p in (0, 3, 4):
                    text_own[r, p] = both
                else:
                    y_send[r, p] = both.astype(jnp.bfloat16)

    def y_send_to(r, p, move):
        send(y_send.at[r, p], y_recv.at[r, p], y_sem.at[r, p], y_peer(move))

    def y_first(r):
        y_send_to(r, 7, 2 - 4 * core)
        y_send_to(r, 6, 1)
        y_send_to(r, 5, -1)
        y_send_to(r, 2, 1)
        y_send_to(r, 1, -1)

    def y_pass(r):
        for p in (5, 6, 7):
            arrived(y_recv.at[r, p], y_sem.at[r, p])
        last = y_recv[r, 7].astype(jnp.float32)
        for p in (3, 4):
            both = text_own[r, p] + y_recv[r, p + 2].astype(jnp.float32)
            both += jnp.where(core == 4 - p, last, jnp.zeros_like(last))
            y_send[r, p] = both.astype(jnp.bfloat16)
            y_send_to(r, p, -moves[p])

    def y_sum(r):
        total = text_own[r, 0]
        for p in range(1, 5):
            arrived(y_recv.at[r, p], y_sem.at[r, p])
            total += y_recv[r, p].astype(jnp.float32)
        return total

    def image_share(k):
        rows = pl.ds(pl.multiple_of(lax.rem(x + k, NX) * x_rows, x_rows), x_rows)
        share = jnp.dot(coef[rows, :], texts[...], preferred_element_type=jnp.float32)
        if k != 2:
            x_full[k] = share
        if k != 0:
            x_half[k] = share.astype(jnp.bfloat16)

    def side_rows(j, side):
        start = (pair_at(j) * 2 + side) * ROWS
        return pl.ds(pl.multiple_of(start, ROWS), ROWS)

    def pass_sends(j):
        for way in range(2):
            send(
                x_half.at[2, side_rows(j, way), :], pass_recv.at[j, way], pass_sem.at[j, way],
                x_peer(1 + 2 * way),
            )

    def x_sends(j):
        for way in range(2):
            send(
                x_half.at[1 + 2 * way, side_rows(j, 1 - way), :], x_recv.at[j, way, 1 - way],
                x_sem.at[j, way, 1 - way], x_peer(1 + 2 * way),
            )

    def pass_on(j):
        for way in range(2):
            arrived(pass_recv.at[j, way], pass_sem.at[j, way])
            both = x_full[1 + 2 * way, side_rows(j, way), :] + pass_recv[j, way].astype(jnp.float32)
            pass_send[j, way] = both.astype(jnp.bfloat16)
            send(
                pass_send.at[j, way], x_recv.at[j, way, way], x_sem.at[j, way, way],
                x_peer(1 + 2 * way),
            )

    def x_sum(j):
        for side in range(2):
            total = x_full[0, side_rows(j, side), :]
            for way in range(2):
                arrived(x_recv.at[j, way, side], x_sem.at[j, way, side])
                total += x_recv[j, way, side].astype(jnp.float32)
            z_own[j, side] = total
        near_send[j] = z_own[j, 1 - z_side].astype(jnp.bfloat16)
        send(near_send.at[j], near_recv.at[j], near_sem.at[j], near)

    def near_sum(j):
        arrived(near_recv.at[j], near_sem.at[j])
        return z_own[j, z_side] + near_recv[j].astype(jnp.float32)

    def middle_sends(j):
        far_send[j] = near_sum(j).astype(jnp.bfloat16)
        send(far_send.at[j], far_recv.at[j], far_sem.at[j], far_peer(1))

    def far_sends():
        total = near_sum(2)
        arrived(far_recv.at[3], far_sem.at[3])
        far_send[2] = (total + far_recv[3].astype(jnp.float32)).astype(jnp.bfloat16)
        send(far_send.at[2], far_recv.at[2], far_sem.at[2], far_peer(2))

    first, second = range(some), range(some, NY)
    order = (3, 4, 1, 2)
    rest = (5, 6, 7)
    take(0, order)
    arrived(place(1, 0, 0), gather_recv.at[1, 0])
    forward(1)
    take(0, rest)
    take(1, order)
    for half, places in enumerate((first, second)):
        take_pair(0, places)
        coefficients(0, half)
        text_share(0, half)
    take(1, rest)
    take_pair(1, first)
    coefficients(1, 0)
    text_share(1, 0)
    take_pair(1, second)
    coefficients(1, 1)

    image_share(2)
    pass_sends(3)
    image_share(1)
    image_share(3)
    x_sends(3)
    text_share(1, 1)
    pass_sends(2)
    pass_on(3)
    pair_sum(1)
    y_first(1)
    x_sends(2)
    image_share(0)
    pair_sum(0)
    pass_sends(1)
    pass_on(2)
    x_sends(1)
    pass_sends(0)
    y_pass(1)
    x_sum(3)
    pass_on(1)
    x_sends(0)
    y_first(0)
    pass_on(0)
    middle_sends(3)
    x_sum(2)
    hi_send[...] = y_sum(1).astype(jnp.bfloat16)
    send(hi_send, hi_recv, hi_sem, opposite)
    x_sum(1)
    y_pass(0)
    far_sends()
    middle_sends(1)
    x_sum(0)
    text_total = y_sum(0)
    total = near_sum(0)
    for j in (1, 2):
        arrived(far_recv.at[j], far_sem.at[j])
        total += far_recv[j].astype(jnp.float32)
    scale = jnp.exp(jnp.full((1, image_in.shape[1]), scale_in[0], jnp.float32))
    own = image_in[pl.ds(pl.multiple_of(group * ROWS, ROWS), ROWS), :].astype(jnp.float32)
    own_norm = inverse_norms(own)
    image_out[...] = norm_backward(own * own_norm, total * scale, own_norm)

    arrived(hi_recv, hi_sem)
    text_total += hi_recv[...].astype(jnp.float32)
    text_out[...] = norm_backward(text_values * text_norm, text_total * scale, text_norm)

    for copy in sent:
        copy.wait_send()


def body(image_embeds, text_embeds, scale_logarithm, logit_bias):
    images, width = image_embeds.shape
    count = NY * 4 * ROWS
    x_rows = NZ * ROWS
    pairs = NZ // 2
    sends = 1 + 4 * NY - 2 + 4 + 2 * NY - 2 + 6 * pairs + 2 * pairs - 1 + 1
    dma = pltpu.SemaphoreType.DMA

    def half(*shape):
        return pltpu.VMEM((*shape, width), jnp.bfloat16)

    def full(*shape):
        return pltpu.VMEM((*shape, width), jnp.float32)

    return pl.pallas_call(
        kernel,
        out_shape=[jax.ShapeDtypeStruct((ROWS, width), jnp.float32)] * 2,
        in_specs=[pl.BlockSpec(memory_space=pl.ANY)] * 4,
        out_specs=[pl.BlockSpec(memory_space=pltpu.VMEM)] * 2,
        scratch_shapes=[
            half(images),
            half(ROWS),
            pltpu.SMEM((1,), jnp.float32),
            pltpu.SMEM((1,), jnp.float32),
            half(images),
            half(count),
            pltpu.VMEM((images, count), jnp.bfloat16),
            pltpu.VMEM((count, images), jnp.bfloat16),
            half(2, 2, NY // 2, ROWS),
            half(2, 2, NY // 2, ROWS),
            full(2, NY, ROWS),
            half(2, NY, ROWS),
            half(2, NY, ROWS),
            half(ROWS),
            half(ROWS),
            full(NX, x_rows),
            half(NX, x_rows),
            half(pairs, 2, ROWS),
            half(pairs, 2, ROWS),
            half(pairs, 2, 2, ROWS),
            full(pairs, 2, ROWS),
            half(pairs, ROWS),
            half(pairs, ROWS),
            half(pairs, ROWS),
            half(pairs, ROWS),
            dma((4,)),
            dma((2, NY)),
            dma((2, NY)),
            dma((2, 2)),
            dma((2, NY)),
            dma,
            dma((pairs, 2)),
            dma((pairs, 2, 2)),
            dma((pairs,)),
            dma((pairs,)),
            dma((sends,)),
        ],
        compiler_params=pltpu.CompilerParams(
            collective_id=0, has_side_effects=True, vmem_limit_bytes=VMEM_BYTES
        ),
        cost_estimate=pl.CostEstimate(
            flops=6 * images * count * width, bytes_accessed=4 * images * width,
            transcendentals=images * count,
        ),
    )(image_embeds, text_embeds, scale_logarithm, logit_bias)


def solution(mesh):
    return jax.shard_map(
        body,
        mesh=mesh,
        in_specs=(P("dp", None), P(("dp", "group"), None), P(), P()),
        out_specs=(P(("dp", "group"), None), P(("dp", "group"), None)),
        check_vma=False,
    )
```

```python
import jax
import jax.numpy as jnp
from jax import lax
from jax.experimental import pallas as pl
from jax.experimental.pallas import tpu as pltpu
from jax.sharding import PartitionSpec as P

NX = 4
NY = 8
NZ = 8
ROWS = 16
VMEM_BYTES = 53 * 1024 * 1024 + 512 * 1024

def offsets(count):
    found = [0]
    for distance in range(1, count // 2 + 1):
        found += [distance, -distance]
    return found[:count]


def inverse_norms(values):
    return lax.rsqrt(jnp.sum(values * values, axis=1, keepdims=True) + 1e-06)


def norm_backward(unit_rows, unit_grad, inverse_norm):
    along = jnp.sum(unit_rows * unit_grad, axis=1, keepdims=True)
    return (unit_grad - unit_rows * along) * inverse_norm


def kernel(
    image_hbm, text_hbm, scale_hbm, bias_hbm, image_out, text_out,
    image_in, text_in, scale_in, bias_in, image_half, texts, coef, coef_text,
    pair_send, pair_recv, text_own, y_send, y_recv, hi_send, hi_recv,
    x_full, x_half, pass_send, pass_recv, x_recv, z_own, near_send, near_recv, far_send, far_recv,
    in_sems, gather_recv, gather_pair_recv, pair_sem, y_sem, hi_sem, pass_sem, x_sem, near_sem, far_sem,
    send_sems,
):
    dp = lax.axis_index("dp")
    group = lax.axis_index("group")
    core = lax.rem(dp, 2)
    y = lax.rem(dp // 2, NY)
    z_hi = dp // (2 * NY)
    x = group // NZ
    z_lo = lax.rem(group, NZ)
    z_pair = z_lo // 2
    z_side = lax.rem(z_lo, 2)
    moves = offsets(NY)
    pairs = NZ // 2
    x_rows = NZ * ROWS
    pair_rows = 2 * ROWS

    def dp_at(z_hi, y, core):
        return (z_hi * NY + y) * 2 + core

    sibling = (dp_at(z_hi, y, 1 - core), group)
    opposite = (dp_at(1 - z_hi, y, core), group)
    near = (dp, x * NZ + z_pair * 2 + 1 - z_side)

    def y_peer(move):
        return (dp_at(z_hi, lax.rem(y + move + NY, NY), core), group)

    def x_peer(k):
        return (dp, lax.rem(x + k, NX) * NZ + z_lo)

    def pair_at(j):
        low, high = lax.rem(z_pair, 2), z_pair // 2
        low = low if j % 2 == 0 else 1 - low
        high = high if j < 2 else 1 - high
        return high * 2 + low

    def far_peer(j):
        return (dp, x * NZ + pair_at(j) * 2 + z_side)

    peers = [opposite, sibling, near]
    peers += [y_peer(move) for move in moves[1:]]
    peers += [x_peer(1), x_peer(3)]
    peers += [far_peer(1), far_peer(2)]
    barrier = pltpu.get_barrier_semaphore()
    for peer in peers:
        pl.semaphore_signal(barrier, inc=1, device_id=peer, device_id_type=pl.DeviceIdType.MESH)

    loads = [
        pltpu.make_async_copy(source, target, in_sems.at[i])
        for i, (source, target) in enumerate(
            [(text_hbm, text_in), (image_hbm, image_in), (scale_hbm, scale_in), (bias_hbm, bias_in)]
        )
    ]
    for load in loads:
        load.start()

    loads[0].wait()
    text_values = text_in[...].astype(jnp.float32)
    text_norm = inverse_norms(text_values)
    texts[pl.ds(0, ROWS), :] = (text_values * text_norm).astype(jnp.bfloat16)

    for load in loads[1:]:
        load.wait()

    @pl.loop(0, NX)
    def _(i):
        rows = pl.ds(pl.multiple_of(i * x_rows, x_rows), x_rows)
        values = image_in[rows, :].astype(jnp.float32)
        image_half[rows, :] = (values * inverse_norms(values)).astype(jnp.bfloat16)

    pl.semaphore_wait(barrier, len(peers))

    started, pending = [], {}

    def send(source, target, arrival, device):
        copy = pltpu.make_async_remote_copy(
            src_ref=source, dst_ref=target, send_sem=send_sems.at[len(started)], recv_sem=arrival,
            device_id=device, device_id_type=pl.DeviceIdType.MESH,
        )
        copy.start()
        pending[len(started)] = copy
        started.append(copy)
        return len(started) - 1

    def arrived(target, arrival):
        pltpu.make_async_copy(target, target, arrival).wait()

    def place(r, p, s):
        start = (r * NY + p) * pair_rows + s * ROWS
        return texts.at[pl.ds(start if isinstance(start, int) else pl.multiple_of(start, ROWS), ROWS), :]

    def gather_send(r, source, target, move):
        send(place(r, source, 0), place(r, target, 0), gather_recv.at[r, target], y_peer(move))

    def forward(r):
        for p in (3, 4, 1, 2) if r == 0 else range(NY - 1, 0, -1):
            gather_send(r, 0, p, moves[p])
        send(place(r, 0, 0), place(r, 0, 1), gather_pair_recv.at[r, 0], sibling)

    def take(r, places):
        for p in places:
            arrived(place(r, p, 0), gather_recv.at[r, p])
            if r == 0 and p == 3:
                gather_send(r, 3, 5, 1)
            elif r == 0 and p == 4:
                gather_send(r, 4, 6, -1)
                gather_send(r, 3 + core, 7, 2 - 4 * core)
            send(place(r, p, 0), place(r, p, 1), gather_pair_recv.at[r, p], sibling)

    def take_pair(r, places):
        for p in places:
            arrived(place(r, p, 1), gather_pair_recv.at[r, p])

    send(place(0, 0, 0), place(1, 0, 0), gather_recv.at[1, 0], opposite)
    forward(0)

    scale_row = jnp.exp(jnp.full((1, image_half.shape[0]), scale_in[0], jnp.float32))
    bias = bias_in[0]
    some = NY // 2
    some_rows = some * pair_rows

    def coefficients(r, half):
        start = (2 * r + half) * some_rows
        logits = lax.dot_general(
            texts[pl.ds(start, some_rows), :], image_half[...], (((1,), (1,)), ((), ())),
            preferred_element_type=jnp.float32,
        ) * scale_row + bias
        if start == 0:
            text_ids = lax.broadcasted_iota(jnp.int32, logits.shape, 0)
            image_ids = lax.broadcasted_iota(jnp.int32, logits.shape, 1)
            same = jnp.logical_and(text_ids < ROWS, image_ids == text_ids + group * ROWS)
            sign = jnp.where(same, jnp.float32(1.0), jnp.float32(-1.0))
            values = -sign / (1.0 + jnp.exp(sign * logits))
        else:
            values = 1.0 / (1.0 + jnp.exp(-logits))
        coef_text[pl.ds(start, some_rows), :] = values.astype(jnp.bfloat16)
        coef[:, pl.ds(start, some_rows)] = values.T.astype(jnp.bfloat16)

    def text_share(r, half):
        share = jnp.dot(
            coef_text[pl.ds((2 * r + half) * some_rows, some_rows), :], image_half[...],
            preferred_element_type=jnp.float32,
        )
        for i in range(some):
            base = i * pair_rows
            text_own[r, half * some + i] = share[base : base + ROWS]
            pair_send[r, half, i] = share[base + ROWS : base + pair_rows].astype(jnp.bfloat16)
        send(pair_send.at[r, half], pair_recv.at[r, half], pair_sem.at[r, half], sibling)

    def pair_sum(r):
        for half in range(1, -1, -1):
            arrived(pair_recv.at[r, half], pair_sem.at[r, half])
            for i in range(some - 1, -1, -1):
                p = half * some + i
                both = text_own[r, p] + pair_recv[r, half, i].astype(jnp.float32)
                if p in (0, 3, 4):
                    text_own[r, p] = both
                else:
                    y_send[r, p] = both.astype(jnp.bfloat16)

    def y_send_to(r, p, move):
        send(y_send.at[r, p], y_recv.at[r, p], y_sem.at[r, p], y_peer(move))

    def y_first(r):
        y_send_to(r, 7, 2 - 4 * core)
        y_send_to(r, 6, 1)
        y_send_to(r, 5, -1)
        y_send_to(r, 2, 1)
        y_send_to(r, 1, -1)

    def y_pass(r):
        for p in (5, 6, 7):
            arrived(y_recv.at[r, p], y_sem.at[r, p])
        last = y_recv[r, 7].astype(jnp.float32)
        for p in (3, 4):
            both = text_own[r, p] + y_recv[r, p + 2].astype(jnp.float32)
            both += jnp.where(core == 4 - p, last, jnp.zeros_like(last))
            y_send[r, p] = both.astype(jnp.bfloat16)
            y_send_to(r, p, -moves[p])

    def y_sum(r):
        total = text_own[r, 0]
        for p in range(1, 5):
            arrived(y_recv.at[r, p], y_sem.at[r, p])
            total += y_recv[r, p].astype(jnp.float32)
        return total

    def image_share(k):
        rows = pl.ds(pl.multiple_of(lax.rem(x + k, NX) * x_rows, x_rows), x_rows)
        share = jnp.dot(coef[rows, :], texts[...], preferred_element_type=jnp.float32)
        if k != 2:
            x_full[k] = share
        if k != 0:
            x_half[k] = share.astype(jnp.bfloat16)

    def side_rows(j, side):
        start = (pair_at(j) * 2 + side) * ROWS
        return pl.ds(pl.multiple_of(start, ROWS), ROWS)

    def pass_sends(j):
        for way in range(2):
            send(
                x_half.at[2, side_rows(j, way), :], pass_recv.at[j, way], pass_sem.at[j, way],
                x_peer(1 + 2 * way),
            )

    going = [[] for _ in range(pairs)]

    def x_sends(j):
        for way in range(2):
            going[j].append(send(
                x_half.at[1 + 2 * way, side_rows(j, 1 - way), :], x_recv.at[j, way, 1 - way],
                x_sem.at[j, way, 1 - way], x_peer(1 + 2 * way),
            ))
        for way in range(2):
            arrived(pass_recv.at[j, way], pass_sem.at[j, way])
            both = x_full[1 + 2 * way, side_rows(j, way), :] + pass_recv[j, way].astype(jnp.float32)
            pass_send[j, way] = both.astype(jnp.bfloat16)
            going[j].append(send(
                pass_send.at[j, way], x_recv.at[j, way, way], x_sem.at[j, way, way],
                x_peer(1 + 2 * way),
            ))

    def settle(j):
        for index in going[j]:
            pending.pop(index).wait_send()

    def x_sum(j):
        for side in range(2):
            total = x_full[0, side_rows(j, side), :]
            for way in range(2):
                arrived(x_recv.at[j, way, side], x_sem.at[j, way, side])
                total += x_recv[j, way, side].astype(jnp.float32)
            z_own[j, side] = total
        near_send[j] = z_own[j, 1 - z_side].astype(jnp.bfloat16)
        send(near_send.at[j], near_recv.at[j], near_sem.at[j], near)

    def near_sum(j):
        arrived(near_recv.at[j], near_sem.at[j])
        return z_own[j, z_side] + near_recv[j].astype(jnp.float32)

    def middle_sends(j):
        far_send[j] = near_sum(j).astype(jnp.bfloat16)
        send(far_send.at[j], far_recv.at[j], far_sem.at[j], far_peer(1))

    def far_sends():
        total = near_sum(2)
        arrived(far_recv.at[3], far_sem.at[3])
        far_send[2] = (total + far_recv[3].astype(jnp.float32)).astype(jnp.bfloat16)
        send(far_send.at[2], far_recv.at[2], far_sem.at[2], far_peer(2))

    first, second = range(some), range(some, NY)
    order = (3, 4, 1, 2)
    rest = (5, 6, 7)
    take(0, order)
    arrived(place(1, 0, 0), gather_recv.at[1, 0])
    forward(1)
    take(0, rest)
    for half, places in enumerate((first, second)):
        take_pair(0, places)
        coefficients(0, half)
        text_share(0, half)
    take(1, range(1, NY))
    take_pair(1, first)
    coefficients(1, 0)
    text_share(1, 0)
    take_pair(1, second)
    coefficients(1, 1)
    text_share(1, 1)

    image_share(2)
    pass_sends(3)
    pass_sends(2)
    pair_sum(1)
    y_first(1)
    image_share(1)
    image_share(3)
    x_sends(3)
    pass_sends(1)
    pair_sum(0)
    image_share(0)
    y_pass(1)
    x_sends(2)
    settle(3)
    pass_sends(0)
    x_sends(1)
    y_first(0)
    x_sum(3)
    settle(2)
    x_sends(0)
    hi_send[...] = y_sum(1).astype(jnp.bfloat16)
    send(hi_send, hi_recv, hi_sem, opposite)
    x_sum(2)
    middle_sends(3)
    y_pass(0)
    x_sum(1)
    far_sends()
    middle_sends(1)
    x_sum(0)
    text_total = y_sum(0)
    total = near_sum(0)
    for j in (1, 2):
        arrived(far_recv.at[j], far_sem.at[j])
        total += far_recv[j].astype(jnp.float32)
    scale = jnp.exp(jnp.full((1, image_in.shape[1]), scale_in[0], jnp.float32))
    own = image_in[pl.ds(pl.multiple_of(group * ROWS, ROWS), ROWS), :].astype(jnp.float32)
    own_norm = inverse_norms(own)
    image_out[...] = norm_backward(own * own_norm, total * scale, own_norm)

    arrived(hi_recv, hi_sem)
    text_total += hi_recv[...].astype(jnp.float32)
    text_out[...] = norm_backward(text_values * text_norm, text_total * scale, text_norm)

    for copy in pending.values():
        copy.wait_send()


def body(image_embeds, text_embeds, scale_logarithm, logit_bias):
    images, width = image_embeds.shape
    count = NY * 4 * ROWS
    x_rows = NZ * ROWS
    pairs = NZ // 2
    sends = 1 + 4 * NY - 2 + 4 + 2 * NY - 2 + 6 * pairs + 2 * pairs - 1 + 1
    dma = pltpu.SemaphoreType.DMA

    def half(*shape):
        return pltpu.VMEM((*shape, width), jnp.bfloat16)

    def full(*shape):
        return pltpu.VMEM((*shape, width), jnp.float32)

    return pl.pallas_call(
        kernel,
        out_shape=[jax.ShapeDtypeStruct((ROWS, width), jnp.float32)] * 2,
        in_specs=[pl.BlockSpec(memory_space=pl.ANY)] * 4,
        out_specs=[pl.BlockSpec(memory_space=pltpu.VMEM)] * 2,
        scratch_shapes=[
            half(images),
            half(ROWS),
            pltpu.SMEM((1,), jnp.float32),
            pltpu.SMEM((1,), jnp.float32),
            half(images),
            half(count),
            pltpu.VMEM((images, count), jnp.bfloat16),
            pltpu.VMEM((count, images), jnp.bfloat16),
            half(2, 2, NY // 2, ROWS),
            half(2, 2, NY // 2, ROWS),
            full(2, NY, ROWS),
            half(2, NY, ROWS),
            half(2, NY, ROWS),
            half(ROWS),
            half(ROWS),
            full(NX, x_rows),
            half(NX, x_rows),
            half(pairs, 2, ROWS),
            half(pairs, 2, ROWS),
            half(pairs, 2, 2, ROWS),
            full(pairs, 2, ROWS),
            half(pairs, ROWS),
            half(pairs, ROWS),
            half(pairs, ROWS),
            half(pairs, ROWS),
            dma((4,)),
            dma((2, NY)),
            dma((2, NY)),
            dma((2, 2)),
            dma((2, NY)),
            dma,
            dma((pairs, 2)),
            dma((pairs, 2, 2)),
            dma((pairs,)),
            dma((pairs,)),
            dma((sends,)),
        ],
        compiler_params=pltpu.CompilerParams(
            collective_id=0, has_side_effects=True, vmem_limit_bytes=VMEM_BYTES
        ),
        cost_estimate=pl.CostEstimate(
            flops=6 * images * count * width, bytes_accessed=4 * images * width,
            transcendentals=images * count,
        ),
    )(image_embeds, text_embeds, scale_logarithm, logit_bias)


def solution(mesh):
    return jax.shard_map(
        body,
        mesh=mesh,
        in_specs=(P("dp", None), P(("dp", "group"), None), P(), P()),
        out_specs=(P(("dp", "group"), None), P(("dp", "group"), None)),
        check_vma=False,
    )
```

```python
import jax
import jax.numpy as jnp
from jax import lax
from jax.experimental import pallas as pl
from jax.experimental.pallas import tpu as pltpu
from jax.sharding import PartitionSpec as P

NX = 4
NY = 8
NZ = 8
ROWS = 16
VMEM_BYTES = 53 * 1024 * 1024 + 512 * 1024

def offsets(count):
    found = [0]
    for distance in range(1, count // 2 + 1):
        found += [distance, -distance]
    return found[:count]


def inverse_norms(values):
    return lax.rsqrt(jnp.sum(values * values, axis=1, keepdims=True) + 1e-06)


def norm_backward(unit_rows, unit_grad, inverse_norm):
    along = jnp.sum(unit_rows * unit_grad, axis=1, keepdims=True)
    return (unit_grad - unit_rows * along) * inverse_norm


def kernel(
    image_hbm, text_hbm, scale_hbm, bias_hbm, image_out, text_out,
    image_in, text_in, scale_in, bias_in, image_half, texts, coef, coef_text,
    pair_send, pair_recv, text_own, y_send, y_recv, hi_send, hi_recv,
    x_full, x_half, pass_send, pass_recv, x_recv, z_own, near_send, near_recv, far_send, far_recv,
    in_sems, gather_recv, gather_pair_recv, pair_sem, y_sem, hi_sem, pass_sem, x_sem, near_sem, far_sem,
    send_sems,
):
    dp = lax.axis_index("dp")
    group = lax.axis_index("group")
    core = lax.rem(dp, 2)
    y = lax.rem(dp // 2, NY)
    z_hi = dp // (2 * NY)
    x = group // NZ
    z_lo = lax.rem(group, NZ)
    z_pair = z_lo // 2
    z_side = lax.rem(z_lo, 2)
    moves = offsets(NY)
    pairs = NZ // 2
    x_rows = NZ * ROWS
    pair_rows = 2 * ROWS

    def dp_at(z_hi, y, core):
        return (z_hi * NY + y) * 2 + core

    sibling = (dp_at(z_hi, y, 1 - core), group)
    opposite = (dp_at(1 - z_hi, y, core), group)
    near = (dp, x * NZ + z_pair * 2 + 1 - z_side)

    def y_peer(move):
        return (dp_at(z_hi, lax.rem(y + move + NY, NY), core), group)

    def x_peer(k):
        return (dp, lax.rem(x + k, NX) * NZ + z_lo)

    def pair_at(j):
        low, high = lax.rem(z_pair, 2), z_pair // 2
        low = low if j % 2 == 0 else 1 - low
        high = high if j < 2 else 1 - high
        return high * 2 + low

    def far_peer(j):
        return (dp, x * NZ + pair_at(j) * 2 + z_side)

    peers = [opposite, sibling, near]
    peers += [y_peer(move) for move in moves[1:]]
    peers += [x_peer(1), x_peer(3)]
    peers += [far_peer(1), far_peer(2)]
    barrier = pltpu.get_barrier_semaphore()
    for peer in peers:
        pl.semaphore_signal(barrier, inc=1, device_id=peer, device_id_type=pl.DeviceIdType.MESH)

    loads = [
        pltpu.make_async_copy(source, target, in_sems.at[i])
        for i, (source, target) in enumerate(
            [(text_hbm, text_in), (image_hbm, image_in), (scale_hbm, scale_in), (bias_hbm, bias_in)]
        )
    ]
    for load in loads:
        load.start()

    loads[0].wait()
    text_values = text_in[...].astype(jnp.float32)
    text_norm = inverse_norms(text_values)
    texts[pl.ds(0, ROWS), :] = (text_values * text_norm).astype(jnp.bfloat16)

    for load in loads[1:]:
        load.wait()

    @pl.loop(0, NX)
    def _(i):
        rows = pl.ds(pl.multiple_of(i * x_rows, x_rows), x_rows)
        values = image_in[rows, :].astype(jnp.float32)
        image_half[rows, :] = (values * inverse_norms(values)).astype(jnp.bfloat16)

    pl.semaphore_wait(barrier, len(peers))

    started, pending = [], {}

    def send(source, target, arrival, device):
        copy = pltpu.make_async_remote_copy(
            src_ref=source, dst_ref=target, send_sem=send_sems.at[len(started)], recv_sem=arrival,
            device_id=device, device_id_type=pl.DeviceIdType.MESH,
        )
        copy.start()
        pending[len(started)] = copy
        started.append(copy)
        return len(started) - 1

    def arrived(target, arrival):
        pltpu.make_async_copy(target, target, arrival).wait()

    def place(r, p, s):
        start = (r * NY + p) * pair_rows + s * ROWS
        return texts.at[pl.ds(start if isinstance(start, int) else pl.multiple_of(start, ROWS), ROWS), :]

    def gather_send(r, source, target, move):
        send(place(r, source, 0), place(r, target, 0), gather_recv.at[r, target], y_peer(move))

    def forward(r):
        for p in (3, 4, 1, 2) if r == 0 else range(NY - 1, 0, -1):
            gather_send(r, 0, p, moves[p])
        send(place(r, 0, 0), place(r, 0, 1), gather_pair_recv.at[r, 0], sibling)

    def take(r, places):
        for p in places:
            arrived(place(r, p, 0), gather_recv.at[r, p])
            if r == 0 and p == 3:
                gather_send(r, 3, 5, 1)
            elif r == 0 and p == 4:
                gather_send(r, 4, 6, -1)
                gather_send(r, 3 + core, 7, 2 - 4 * core)
            send(place(r, p, 0), place(r, p, 1), gather_pair_recv.at[r, p], sibling)

    def take_pair(r, places):
        for p in places:
            arrived(place(r, p, 1), gather_pair_recv.at[r, p])

    send(place(0, 0, 0), place(1, 0, 0), gather_recv.at[1, 0], opposite)
    forward(0)

    scale_row = jnp.exp(jnp.full((1, image_half.shape[0]), scale_in[0], jnp.float32))
    bias = bias_in[0]
    some = NY // 2
    some_rows = some * pair_rows

    def coefficients(r, half):
        start = (2 * r + half) * some_rows
        logits = lax.dot_general(
            texts[pl.ds(start, some_rows), :], image_half[...], (((1,), (1,)), ((), ())),
            preferred_element_type=jnp.float32,
        ) * scale_row + bias
        if start == 0:
            text_ids = lax.broadcasted_iota(jnp.int32, logits.shape, 0)
            image_ids = lax.broadcasted_iota(jnp.int32, logits.shape, 1)
            same = jnp.logical_and(text_ids < ROWS, image_ids == text_ids + group * ROWS)
            sign = jnp.where(same, jnp.float32(1.0), jnp.float32(-1.0))
            values = -sign / (1.0 + jnp.exp(sign * logits))
        else:
            values = 1.0 / (1.0 + jnp.exp(-logits))
        coef_text[pl.ds(start, some_rows), :] = values.astype(jnp.bfloat16)
        coef[:, pl.ds(start, some_rows)] = values.T.astype(jnp.bfloat16)

    def text_share(r, half):
        share = jnp.dot(
            coef_text[pl.ds((2 * r + half) * some_rows, some_rows), :], image_half[...],
            preferred_element_type=jnp.float32,
        )
        for i in range(some):
            base = i * pair_rows
            text_own[r, half * some + i] = share[base : base + ROWS]
            pair_send[r, half, i] = share[base + ROWS : base + pair_rows].astype(jnp.bfloat16)
        send(pair_send.at[r, half], pair_recv.at[r, half], pair_sem.at[r, half], sibling)

    def pair_sum(r):
        for half in range(1, -1, -1):
            arrived(pair_recv.at[r, half], pair_sem.at[r, half])
            for i in range(some - 1, -1, -1):
                p = half * some + i
                both = text_own[r, p] + pair_recv[r, half, i].astype(jnp.float32)
                if p in (0, 3, 4):
                    text_own[r, p] = both
                else:
                    y_send[r, p] = both.astype(jnp.bfloat16)

    def y_send_to(r, p, move):
        send(y_send.at[r, p], y_recv.at[r, p], y_sem.at[r, p], y_peer(move))

    def y_first(r):
        y_send_to(r, 7, 2 - 4 * core)
        y_send_to(r, 6, 1)
        y_send_to(r, 5, -1)
        y_send_to(r, 2, 1)
        y_send_to(r, 1, -1)

    def y_pass(r):
        for p in (5, 6, 7):
            arrived(y_recv.at[r, p], y_sem.at[r, p])
        last = y_recv[r, 7].astype(jnp.float32)
        for p in (3, 4):
            both = text_own[r, p] + y_recv[r, p + 2].astype(jnp.float32)
            both += jnp.where(core == 4 - p, last, jnp.zeros_like(last))
            y_send[r, p] = both.astype(jnp.bfloat16)
            y_send_to(r, p, -moves[p])

    def y_sum(r):
        total = text_own[r, 0]
        for p in range(1, 5):
            arrived(y_recv.at[r, p], y_sem.at[r, p])
            total += y_recv[r, p].astype(jnp.float32)
        return total

    def image_share(k):
        rows = pl.ds(pl.multiple_of(lax.rem(x + k, NX) * x_rows, x_rows), x_rows)
        share = jnp.dot(coef[rows, :], texts[...], preferred_element_type=jnp.float32)
        if k != 2:
            x_full[k] = share
        if k != 0:
            x_half[k] = share.astype(jnp.bfloat16)

    def side_rows(j, side):
        start = (pair_at(j) * 2 + side) * ROWS
        return pl.ds(pl.multiple_of(start, ROWS), ROWS)

    def pass_sends(j):
        for way in range(2):
            send(
                x_half.at[2, side_rows(j, way), :], pass_recv.at[j, way], pass_sem.at[j, way],
                x_peer(1 + 2 * way),
            )

    going = [[] for _ in range(pairs)]

    def x_sends(j):
        for way in range(2):
            going[j].append(send(
                x_half.at[1 + 2 * way, side_rows(j, 1 - way), :], x_recv.at[j, way, 1 - way],
                x_sem.at[j, way, 1 - way], x_peer(1 + 2 * way),
            ))
        for way in range(2):
            arrived(pass_recv.at[j, way], pass_sem.at[j, way])
            both = x_full[1 + 2 * way, side_rows(j, way), :] + pass_recv[j, way].astype(jnp.float32)
            pass_send[j, way] = both.astype(jnp.bfloat16)
            going[j].append(send(
                pass_send.at[j, way], x_recv.at[j, way, way], x_sem.at[j, way, way],
                x_peer(1 + 2 * way),
            ))

    def settle(j):
        for index in going[j]:
            pending.pop(index).wait_send()

    def x_sum(j):
        for side in range(2):
            total = x_full[0, side_rows(j, side), :]
            for way in range(2):
                arrived(x_recv.at[j, way, side], x_sem.at[j, way, side])
                total += x_recv[j, way, side].astype(jnp.float32)
            z_own[j, side] = total
        near_send[j] = z_own[j, 1 - z_side].astype(jnp.bfloat16)
        send(near_send.at[j], near_recv.at[j], near_sem.at[j], near)

    def near_sum(j):
        arrived(near_recv.at[j], near_sem.at[j])
        return z_own[j, z_side] + near_recv[j].astype(jnp.float32)

    def middle_sends(j):
        far_send[j] = near_sum(j).astype(jnp.bfloat16)
        send(far_send.at[j], far_recv.at[j], far_sem.at[j], far_peer(1))

    def far_sends():
        total = near_sum(2)
        arrived(far_recv.at[3], far_sem.at[3])
        far_send[2] = (total + far_recv[3].astype(jnp.float32)).astype(jnp.bfloat16)
        send(far_send.at[2], far_recv.at[2], far_sem.at[2], far_peer(2))

    first, second = range(some), range(some, NY)
    order = (3, 4, 1, 2)
    rest = (5, 6, 7)
    take(0, order)
    arrived(place(1, 0, 0), gather_recv.at[1, 0])
    forward(1)
    take(0, rest)
    for half, places in enumerate((first, second)):
        take_pair(0, places)
        coefficients(0, half)
        text_share(0, half)
    take(1, range(1, NY))
    take_pair(1, first)
    coefficients(1, 0)
    text_share(1, 0)
    take_pair(1, second)
    coefficients(1, 1)
    text_share(1, 1)

    image_share(2)
    pass_sends(3)
    pass_sends(2)
    pair_sum(1)
    y_first(1)
    image_share(1)
    image_share(3)
    x_sends(3)
    pass_sends(1)
    pair_sum(0)
    image_share(0)
    y_pass(1)
    x_sends(2)
    settle(3)
    pass_sends(0)
    x_sends(1)
    y_first(0)
    x_sum(3)
    settle(2)
    x_sends(0)
    middle_sends(3)
    hi_send[...] = y_sum(1).astype(jnp.bfloat16)
    send(hi_send, hi_recv, hi_sem, opposite)
    x_sum(2)
    y_pass(0)
    x_sum(1)
    far_sends()
    middle_sends(1)
    x_sum(0)
    text_total = y_sum(0)
    total = near_sum(0)
    for j in (1, 2):
        arrived(far_recv.at[j], far_sem.at[j])
        total += far_recv[j].astype(jnp.float32)
    scale = jnp.exp(jnp.full((1, image_in.shape[1]), scale_in[0], jnp.float32))
    own = image_in[pl.ds(pl.multiple_of(group * ROWS, ROWS), ROWS), :].astype(jnp.float32)
    own_norm = inverse_norms(own)
    image_out[...] = norm_backward(own * own_norm, total * scale, own_norm)

    arrived(hi_recv, hi_sem)
    text_total += hi_recv[...].astype(jnp.float32)
    text_out[...] = norm_backward(text_values * text_norm, text_total * scale, text_norm)

    for copy in pending.values():
        copy.wait_send()


def body(image_embeds, text_embeds, scale_logarithm, logit_bias):
    images, width = image_embeds.shape
    count = NY * 4 * ROWS
    x_rows = NZ * ROWS
    pairs = NZ // 2
    sends = 1 + 4 * NY - 2 + 4 + 2 * NY - 2 + 6 * pairs + 2 * pairs - 1 + 1
    dma = pltpu.SemaphoreType.DMA

    def half(*shape):
        return pltpu.VMEM((*shape, width), jnp.bfloat16)

    def full(*shape):
        return pltpu.VMEM((*shape, width), jnp.float32)

    return pl.pallas_call(
        kernel,
        out_shape=[jax.ShapeDtypeStruct((ROWS, width), jnp.float32)] * 2,
        in_specs=[pl.BlockSpec(memory_space=pl.ANY)] * 4,
        out_specs=[pl.BlockSpec(memory_space=pltpu.VMEM)] * 2,
        scratch_shapes=[
            half(images),
            half(ROWS),
            pltpu.SMEM((1,), jnp.float32),
            pltpu.SMEM((1,), jnp.float32),
            half(images),
            half(count),
            pltpu.VMEM((images, count), jnp.bfloat16),
            pltpu.VMEM((count, images), jnp.bfloat16),
            half(2, 2, NY // 2, ROWS),
            half(2, 2, NY // 2, ROWS),
            full(2, NY, ROWS),
            half(2, NY, ROWS),
            half(2, NY, ROWS),
            half(ROWS),
            half(ROWS),
            full(NX, x_rows),
            half(NX, x_rows),
            half(pairs, 2, ROWS),
            half(pairs, 2, ROWS),
            half(pairs, 2, 2, ROWS),
            full(pairs, 2, ROWS),
            half(pairs, ROWS),
            half(pairs, ROWS),
            half(pairs, ROWS),
            half(pairs, ROWS),
            dma((4,)),
            dma((2, NY)),
            dma((2, NY)),
            dma((2, 2)),
            dma((2, NY)),
            dma,
            dma((pairs, 2)),
            dma((pairs, 2, 2)),
            dma((pairs,)),
            dma((pairs,)),
            dma((sends,)),
        ],
        compiler_params=pltpu.CompilerParams(
            collective_id=0, has_side_effects=True, vmem_limit_bytes=VMEM_BYTES
        ),
        cost_estimate=pl.CostEstimate(
            flops=6 * images * count * width, bytes_accessed=4 * images * width,
            transcendentals=images * count,
        ),
    )(image_embeds, text_embeds, scale_logarithm, logit_bias)


def solution(mesh):
    return jax.shard_map(
        body,
        mesh=mesh,
        in_specs=(P("dp", None), P(("dp", "group"), None), P(), P()),
        out_specs=(P(("dp", "group"), None), P(("dp", "group"), None)),
        check_vma=False,
    )
```
